32 devices in a mesh: row: 4 (over y, x), col: 8 (over z, core).
Axes of the slice: x: 2, y: 2, z: 4, core: 2. Of those that a mesh axis runs over, the one named last changes fastest.
Arguments:
- anomalies: bfloat16 [128, 256, 1024], P('row', 'col'), may hold values from -6 to 6
- kappa: bfloat16 [128, 256], P('row', 'col'), may hold values from 0.039794922 to 0.23925781
- members: int32 [1024], replicated, may hold values from 0 to 7
- months: int32 [1024], replicated, may hold values from 0 to 11
- land: int32 [128, 256], P('row', 'col'), may hold values 0 or 1
Outputs:
- covariance: bfloat16 [32768, 32768], P('row', 'col')
The draws below stay inside these ranges and needn't reach their ends.
All inputs are finite; a program needn't handle non-finite values. No bound on the sum of `land` on one device may be relied on, other than what follows from the above.
Results may differ from the reference program's by a relative error of at most 0.0053.
Values may be sent and summed in bfloat16 or wider, within the bound.
A program may use at most 192 MiB of HBM per device.

```python
import math
import jax
import jax.numpy as jnp
from jax import lax

LAT = 128
LON = 256
MAPS = 1024
MEMBERS = 8
MONTHS = 12
STEPS = 4
TILE = 2048
GROUPS = 96


def touch_ends(values, stream_key, least, largest):
    longest = values.shape.index(max(values.shape))
    spots = []
    for shift in (0, 1):
        where = [jax.random.randint(jax.random.fold_in(stream_key, axis), (), 0, length) for axis, length in enumerate(values.shape)]
        where[longest] = (where[longest] + shift) % values.shape[longest]
        spots.append(tuple(where))
    return values.at[spots[0]].set(least).at[spots[1]].set(largest)


def shard_levels(stream_key, extent, shards, least, largest):
    def one(position, shards_of):
        steps = jax.random.uniform(jax.random.fold_in(jax.random.fold_in(stream_key, 6), position), (shards_of,), jnp.float32, least / len(shards), largest / len(shards))
        return jnp.repeat(jnp.exp(steps), extent[position] // shards_of).reshape((-1,) + (1,) * (len(extent) - position - 1))

    gain = one(*shards[0])
    for cut in shards[1:]:
        gain = gain * one(*cut)
    return gain


def noise(rng, extent, deviation, bound, pieces=(), kind=jnp.bfloat16):
    loudness = shard_levels(rng, extent, pieces, -0.22, 0.18) if pieces else 1.0
    values = jax.random.normal(rng, extent, jnp.float32) * deviation * loudness
    return jnp.minimum(jnp.maximum(values, -bound), bound).astype(kind)


def setup_inputs(seed: int = 0) -> dict:
    key_of = jax.random.split(jax.random.key(seed), 6)
    return {
        "anomalies": noise(key_of[0], (LAT, LON, MAPS), 1.0, 6.0, ((0, 4), (1, 8))),
        "kappa": jnp.clip(jnp.exp(math.log(0.23925781) - 1.7938024 * jax.random.uniform(key_of[1], (LAT, LON), jnp.float32) ** shard_levels(key_of[1], (LAT, LON), ((0, 4), (1, 8)), -0.2, 0.2)), 0.039794922, 0.23925781).astype(jnp.bfloat16),
        "members": touch_ends(jax.random.randint(key_of[2], (MAPS,), 0, MEMBERS), jax.random.fold_in(key_of[2], 1), 0, MEMBERS - 1).astype(jnp.int32),
        "months": touch_ends(jax.random.randint(key_of[3], (MAPS,), 0, MONTHS), jax.random.fold_in(key_of[3], 1), 0, MONTHS - 1).astype(jnp.int32),
        "land": touch_ends((jax.random.randint(key_of[4], (LAT, LON), 0, 10) < 3).astype(jnp.int32), jax.random.fold_in(key_of[4], 1), 0, 1),
    }


def reference(anomalies, kappa, members, months, land):
    field = anomalies.astype(jnp.float32)
    coeff = kappa.astype(jnp.float32)[:, :, None]
    for step in range(STEPS):
        padded = jnp.pad(field, ((1, 1), (0, 0), (0, 0)))
        beside = padded[2:] + padded[:-2] + (jnp.roll(field, -1, axis=1) + jnp.roll(field, 1, axis=1))
        field = field + coeff * (beside - 4.0 * field)
    groups = members * MONTHS + months
    onehot = (groups[:, None] == jnp.arange(GROUPS, dtype=jnp.int32)[None, :]).astype(jnp.float32)
    flat = field.reshape(LAT * LON, MAPS)
    sums = jnp.dot(flat, onehot, precision=lax.Precision.HIGHEST)
    counts = jnp.maximum(lax.optimization_barrier(jnp.sum(onehot, axis=0)), 1.0)
    back = jnp.dot(sums / counts, onehot.T, precision=lax.Precision.HIGHEST)
    phi = ((jnp.arange(LAT).astype(jnp.float32) + 0.5) / LAT - 0.5) * math.pi
    lat_weight = jnp.sqrt(jnp.cos(phi))
    sea_weight = jnp.where(land == 1, 1.0, 0.5).astype(jnp.float32)
    weights = (sea_weight * lat_weight[:, None]).reshape(LAT * LON, 1)
    centred = ((flat - back) * weights).astype(jnp.bfloat16)
    wide = centred.astype(jnp.float32)
    col_tile = jnp.arange(LAT * LON, dtype=jnp.int32) // TILE

    def tile_row(index):
        rows = lax.dynamic_slice_in_dim(wide, (index * TILE).astype(jnp.int32), TILE, 0)
        block = jnp.dot(rows, wide.T, precision=lax.Precision.HIGHEST) / MAPS
        block = jnp.where(col_tile[None, :] >= index, block, 0.0)
        return block.astype(jnp.bfloat16)
    stacked = lax.map(tile_row, jnp.arange(16, dtype=jnp.int32))
    return stacked.reshape(LAT * LON, LAT * LON)
```

```python
import functools
import math

import jax
import jax.numpy as jnp
from jax import lax
from jax.experimental import pallas as pl
from jax.experimental.pallas import tpu as pltpu
from jax.sharding import PartitionSpec as P

LAT = 128
MONTHS = 12
STEPS = 4
TILE = 2048
GROUPS = 96
MESH = pl.DeviceIdType.MESH
VMEM_LIMIT = 56 * 1024 * 1024


def extended(array, axis, dim, width, wrap):
    size, length = (lax.axis_size(axis), array.shape[dim])
    up = [(i, (i + 1) % size) for i in range(size if wrap else size - 1)]
    down = [(j, i) for i, j in up]
    last = lax.slice_in_dim(array, length - width, length, axis=dim)
    first = lax.slice_in_dim(array, 0, width, axis=dim)
    before = lax.ppermute(last, axis, up)
    after = lax.ppermute(first, axis, down)
    return jnp.concatenate([before, array, after], axis=dim)


def centre_maps(field, weights, onehot, counts):
    lat_rows, lon_cols, maps = field.shape
    flat = field.reshape(lat_rows * lon_cols, maps)
    sums = jnp.dot(flat, onehot, precision=lax.Precision.HIGHEST)
    back = jnp.dot(sums / counts, onehot.T, precision=lax.Precision.HIGHEST)
    centred = ((flat - back) * weights.reshape(lat_rows * lon_cols, 1)).astype(jnp.bfloat16)
    return centred.reshape(lat_rows, lon_cols, maps)


def ring_place(r, size):
    half = size // 2
    return jnp.where(r % 2 == 0, r // 2, size - 1 - r // 2), half


def ring_row(place, size):
    place = lax.rem(place + size, size)
    return jnp.where(place < size // 2, 2 * place, 2 * (size - 1 - place) + 1)


def gather_kernel(
    rows, chips, tile_lats, x, band, panel,
    local_sem, root_sem, chain_send, chain_recv, pair_send, pair_recv, ring_send, ring_recv,
):
    r = lax.axis_index("row")
    c = lax.axis_index("col")
    z = c // 2
    k = c % 2
    tiles = x.shape[0] // tile_lats
    mine = tiles // 2
    part = tile_lats // 2
    slots = tiles * chips
    lag = 2
    place, _ = ring_place(r, rows)
    root_place, _ = ring_place(z, rows)
    ring_to = (ring_row(place + 1, rows), ring_row(place - 1, rows))
    hops = (lax.rem(place - root_place + rows, rows), lax.rem(root_place - place + rows, rows))
    is_root = r == z
    has_next = (z < chips - 1, z > 0)
    step = (1, -1)

    def signal(row, col):
        pl.semaphore_signal(barrier, inc=1, device_id=(row, col), device_id_type=MESH)

    barrier = pltpu.get_barrier_semaphore()
    signal(r, 2 * z + 1 - k)
    signal(ring_to[0], c)
    signal(ring_to[1], c)
    for way in range(2):
        @pl.when(has_next[way])
        def _(way=way):
            signal(r, c + 2 * step[way])
    pl.semaphore_wait(
        barrier, 3 + has_next[0].astype(jnp.int32) + has_next[1].astype(jnp.int32))

    def slot_of(i):
        j = i // chips
        return (j % 2) * mine + j // 2, i % chips

    def lats(q):
        return pl.ds(q * tile_lats, tile_lats)

    def source_chip(way, t):
        return z - step[way] * t

    def valid(way, t):
        chip = source_chip(way, t)
        ok = jnp.logical_and(chip >= 0, chip < chips)
        return ok if way == 0 else jnp.logical_and(ok, t > 0)

    def local(q):
        return pltpu.make_async_copy(x.at[lats(q)], band.at[lats(q), c], local_sem.at[q])

    def chain(way, q, t, own):
        block = 2 * source_chip(way, t) + k
        return pltpu.make_async_remote_copy(
            src_ref=x.at[lats(q)] if own else band.at[lats(q), block],
            dst_ref=band.at[lats(q), block],
            send_sem=chain_send.at[way, q, t],
            recv_sem=chain_recv.at[way, q, t],
            device_id=(r, c + 2 * step[way]),
            device_id_type=MESH,
        )

    def pair(way, q, t, own):
        block = 2 * source_chip(way, t) + k
        return pltpu.make_async_remote_copy(
            src_ref=x.at[lats(q)] if own else band.at[lats(q), block],
            dst_ref=band.at[lats(q), block],
            send_sem=pair_send.at[way, q, t],
            recv_sem=pair_recv.at[way, q, t],
            device_id=(r, 2 * z + 1 - k),
            device_id_type=MESH,
        )

    def ring(turn, way, q, t, root):
        chip = source_chip(way, t)
        first = (q - k * mine) * tile_lats + turn * part
        here = panel.at[pl.ds(first, part), pl.ds(2 * chip, 2)]
        origin = band.at[pl.ds(q * tile_lats + turn * part, part), pl.ds(2 * chip, 2)]
        return pltpu.make_async_remote_copy(
            src_ref=origin if root else here,
            dst_ref=here,
            send_sem=ring_send.at[turn, way, q, t],
            recv_sem=ring_recv.at[turn, way, q, t],
            device_id=(ring_to[turn], c),
            device_id_type=MESH,
        )

    def root_copy(way, q, t):
        chip = source_chip(way, t)
        return pltpu.make_async_copy(
            band.at[lats(q), pl.ds(2 * chip, 2)],
            panel.at[pl.ds((q - k * mine) * tile_lats, tile_lats), pl.ds(2 * chip, 2)],
            root_sem.at[way, q, t],
        )

    def chain_slot(i):
        q, t = slot_of(i)

        @pl.when(t == 0)
        def _():
            local(q).start()
            for way in range(2):
                @pl.when(has_next[way])
                def _(way=way):
                    chain(way, q, 0, True).start()
            pair(0, q, 0, True).start()

        for way in range(2):
            @pl.when(jnp.logical_and(t > 0, valid(way, t)))
            def _(way=way):
                chain(way, q, t - 1, False).wait_recv()

                @pl.when(has_next[way])
                def _():
                    chain(way, q, t, False).start()
                pair(way, q, t, False).start()

    def used(way, q, t):
        return jnp.logical_and(valid(way, t), q // mine == k)

    def root_slot(i):
        q, t = slot_of(i)
        for way in range(2):
            @pl.when(valid(way, t))
            def _(way=way):
                pair(way, q, t, False).wait_recv()

                @pl.when(jnp.logical_and(way == 0, t == 0))
                def _():
                    local(q).wait()

                @pl.when(q // mine == k)
                def _():
                    for turn in range(2):
                        ring(turn, way, q, t, True).start()
                    root_copy(way, q, t).start()

    def leaf_slot(i):
        q, t = slot_of(i)
        for way in range(2):
            @pl.when(used(way, q, t))
            def _(way=way):
                for turn in range(2):
                    ring(turn, way, q, t, False).wait_recv()

                    @pl.when(hops[turn] < rows - 1)
                    def _(turn=turn):
                        ring(turn, way, q, t, False).start()

    @pl.loop(0, slots + lag)
    def _(i):
        @pl.when(i < slots)
        def _():
            chain_slot(i)

            @pl.when(is_root)
            def _():
                root_slot(i)

        @pl.when(jnp.logical_and(i >= lag, jnp.logical_not(is_root)))
        def _():
            leaf_slot(i - lag)

    @pl.loop(0, slots)
    def _(i):
        q, t = slot_of(i)

        @pl.when(jnp.logical_and(t == 0, jnp.logical_not(is_root)))
        def _():
            local(q).wait()

        for way in range(2):
            @pl.when(jnp.logical_and(has_next[way], jnp.logical_or(valid(way, t), t == 0)))
            def _(way=way):
                chain(way, q, t, False).wait_send()

            @pl.when(valid(way, t))
            def _(way=way):
                pair(way, q, t, False).wait_send()

                @pl.when(jnp.logical_not(is_root))
                def _():
                    pair(way, q, t, False).wait_recv()

            @pl.when(used(way, q, t))
            def _(way=way):
                for turn in range(2):
                    @pl.when(jnp.logical_or(is_root, hops[turn] < rows - 1))
                    def _(turn=turn):
                        ring(turn, way, q, t, False).wait_send()

                @pl.when(is_root)
                def _():
                    root_copy(way, q, t).wait()


def gather(block, tile_lats, panel_lats):
    rows, cols = lax.axis_size("row"), lax.axis_size("col")
    chips = cols // 2
    lat_rows, lon_cols, maps = block.shape
    tiles = lat_rows // tile_lats
    sems = pltpu.SemaphoreType.DMA
    hbm = pl.BlockSpec(memory_space=pltpu.HBM)
    return pl.pallas_call(
        functools.partial(gather_kernel, rows, chips, tile_lats),
        out_shape=(
            jax.ShapeDtypeStruct((lat_rows, cols, lon_cols, maps), block.dtype),
            jax.ShapeDtypeStruct((panel_lats, cols, lon_cols, maps), block.dtype),
        ),
        in_specs=[hbm],
        out_specs=(hbm, hbm),
        scratch_shapes=[
            sems((tiles,)),
            sems((2, tiles, chips)),
            sems((2, tiles, chips)),
            sems((2, tiles, chips)),
            sems((2, tiles, chips)),
            sems((2, tiles, chips)),
            sems((2, 2, tiles, chips)),
            sems((2, 2, tiles, chips)),
        ],
        compiler_params=pltpu.CompilerParams(collective_id=0, has_side_effects=True),
        name="gather_maps",
    )(block)


def product_kernel(row_tile_count, col_tile_count, strip, wide, left, right, out):
    row = lax.axis_index("row") * row_tile_count + pl.program_id(0) * strip // TILE
    first_col = lax.axis_index("col") * col_tile_count
    scale = 1.0 / left.shape[1]

    @pl.loop(0, out.shape[1] // wide)
    def _(j):
        at = pl.ds(pl.multiple_of(j * wide, wide), wide)
        keep = first_col + j * wide // TILE >= row

        @pl.when(keep)
        def _():
            acc = lax.dot_general(
                left[...], right[at, :], (((1,), (1,)), ((), ())),
                preferred_element_type=jnp.float32)
            out[:, at] = (acc * scale).astype(out.dtype)

        @pl.when(jnp.logical_not(keep))
        def _():
            out[:, at] = jnp.zeros((out.shape[0], wide), out.dtype)


def product(left, right):
    rows, maps = left.shape
    cols = right.shape[0]
    strip, wide = 512, 1024
    return pl.pallas_call(
        functools.partial(product_kernel, rows // TILE, cols // TILE, strip, wide),
        grid=(rows // strip,),
        out_shape=jax.ShapeDtypeStruct((rows, cols), jnp.bfloat16),
        in_specs=[
            pl.BlockSpec((strip, maps), lambda i: (i, 0)),
            pl.BlockSpec((cols, maps), lambda i: (0, 0)),
        ],
        out_specs=pl.BlockSpec((strip, cols), lambda i: (i, 0)),
        compiler_params=pltpu.CompilerParams(vmem_limit_bytes=VMEM_LIMIT),
        name="covariance_product",
    )(left, right)


def per_device(anomalies, kappa, members, months, land):
    lat_rows, lon_cols, maps = anomalies.shape
    row_index = lax.axis_index("row")
    lat_ids = row_index * lat_rows + jnp.arange(lat_rows, dtype=jnp.int32)
    phi = ((lat_ids.astype(jnp.float32) + 0.5) / LAT - 0.5) * math.pi
    lat_weight = jnp.sqrt(jnp.cos(phi))
    sea_weight = jnp.where(land == 1, 1.0, 0.5).astype(jnp.float32)
    cell_weight = sea_weight * lat_weight[:, None]
    groups = members * MONTHS + months
    onehot = (groups[:, None] == jnp.arange(GROUPS, dtype=jnp.int32)[None, :]).astype(jnp.float32)
    counts = jnp.maximum(jnp.sum(onehot, axis=0), 1.0)
    field = extended(anomalies, "col", 1, STEPS, True)
    field = extended(field, "row", 0, STEPS, False).astype(jnp.float32)
    coeff = extended(extended(kappa, "col", 1, STEPS, True), "row", 0, STEPS, False)
    coeff = coeff.astype(jnp.float32)[:, :, None]
    for step in range(STEPS):
        inner = field[1:-1, 1:-1]
        coeff = coeff[1:-1, 1:-1]
        beside = field[2:, 1:-1] + field[:-2, 1:-1] + (field[1:-1, 2:] + field[1:-1, :-2])
        field = inner + coeff * (beside - 4.0 * inner)
    block = centre_maps(field, cell_weight, onehot, counts)
    lon = lon_cols * lax.axis_size("col")
    panel_lats = lat_rows * lax.axis_size("row") // lax.axis_size("col")
    band, panel = gather(block, TILE // lon, panel_lats)
    return product(band.reshape(-1, maps), panel.reshape(-1, maps))


def solution(mesh):
    placed = (P("row", "col", None), P("row", "col"), P(), P(), P("row", "col"))
    return jax.shard_map(
        per_device, mesh=mesh, in_specs=placed, out_specs=P("row", "col"), check_vma=False
    )
```

```python
import functools
import math

import jax
import jax.numpy as jnp
from jax import lax
from jax.experimental import pallas as pl
from jax.experimental.pallas import tpu as pltpu
from jax.sharding import PartitionSpec as P

LAT = 128
MONTHS = 12
STEPS = 4
TILE = 2048
GROUPS = 96
MESH = pl.DeviceIdType.MESH
VMEM_LIMIT = 56 * 1024 * 1024


def extended(array, axis, dim, width, wrap):
    size, length = (lax.axis_size(axis), array.shape[dim])
    up = [(i, (i + 1) % size) for i in range(size if wrap else size - 1)]
    down = [(j, i) for i, j in up]
    last = lax.slice_in_dim(array, length - width, length, axis=dim)
    first = lax.slice_in_dim(array, 0, width, axis=dim)
    before = lax.ppermute(last, axis, up)
    after = lax.ppermute(first, axis, down)
    return jnp.concatenate([before, array, after], axis=dim)


def centre_maps(field, weights, onehot, counts):
    lat_rows, lon_cols, maps = field.shape
    flat = field.reshape(lat_rows * lon_cols, maps)
    sums = jnp.dot(flat, onehot, precision=lax.Precision.HIGHEST)
    back = jnp.dot(sums / counts, onehot.T, precision=lax.Precision.HIGHEST)
    centred = ((flat - back) * weights.reshape(lat_rows * lon_cols, 1)).astype(jnp.bfloat16)
    return centred.reshape(lat_rows, lon_cols, maps)


def ring_place(r, size):
    half = size // 2
    return jnp.where(r % 2 == 0, r // 2, size - 1 - r // 2), half


def ring_row(place, size):
    place = lax.rem(place + size, size)
    return jnp.where(place < size // 2, 2 * place, 2 * (size - 1 - place) + 1)


def gather_kernel(
    rows, chips, tile_lats, x, band, panel,
    local_sem, root_sem, chain_send, chain_recv, pair_send, pair_recv, ring_send, ring_recv,
):
    r = lax.axis_index("row")
    c = lax.axis_index("col")
    z = c // 2
    k = c % 2
    tiles = x.shape[0] // tile_lats
    mine = tiles // 2
    part = tile_lats // 2
    slots = tiles * chips
    spread = 2
    place, _ = ring_place(r, rows)
    root_place, _ = ring_place(z, rows)
    ring_to = (ring_row(place + 1, rows), ring_row(place - 1, rows))
    hops = (lax.rem(place - root_place + rows, rows), lax.rem(root_place - place + rows, rows))
    is_root = r == z
    has_next = (z < chips - 1, z > 0)
    step = (1, -1)

    def signal(row, col):
        pl.semaphore_signal(barrier, inc=1, device_id=(row, col), device_id_type=MESH)

    barrier = pltpu.get_barrier_semaphore()
    signal(r, 2 * z + 1 - k)
    signal(ring_to[0], c)
    signal(ring_to[1], c)
    for way in range(2):
        @pl.when(has_next[way])
        def _(way=way):
            signal(r, c + 2 * step[way])
    pl.semaphore_wait(
        barrier, 3 + has_next[0].astype(jnp.int32) + has_next[1].astype(jnp.int32))

    def slot_of(i):
        j = i // chips
        return (j % 2) * mine + j // 2, i % chips

    def lats(q):
        return pl.ds(q * tile_lats, tile_lats)

    def source_chip(way, t):
        return z - step[way] * t

    def valid(way, t):
        chip = source_chip(way, t)
        ok = jnp.logical_and(chip >= 0, chip < chips)
        return ok if way == 0 else jnp.logical_and(ok, t > 0)

    def local(q):
        return pltpu.make_async_copy(x.at[lats(q)], band.at[lats(q), c], local_sem.at[q])

    def chain(way, q, t, own):
        block = 2 * source_chip(way, t) + k
        return pltpu.make_async_remote_copy(
            src_ref=x.at[lats(q)] if own else band.at[lats(q), block],
            dst_ref=band.at[lats(q), block],
            send_sem=chain_send.at[way, q, t],
            recv_sem=chain_recv.at[way, q, t],
            device_id=(r, c + 2 * step[way]),
            device_id_type=MESH,
        )

    def pair(way, q, t, own):
        block = 2 * source_chip(way, t) + k
        return pltpu.make_async_remote_copy(
            src_ref=x.at[lats(q)] if own else band.at[lats(q), block],
            dst_ref=band.at[lats(q), block],
            send_sem=pair_send.at[way, q, t],
            recv_sem=pair_recv.at[way, q, t],
            device_id=(r, 2 * z + 1 - k),
            device_id_type=MESH,
        )

    def ring(turn, way, q, t, root):
        chip = source_chip(way, t)
        first = (q - k * mine) * tile_lats + turn * part
        here = panel.at[pl.ds(first, part), pl.ds(2 * chip, 2)]
        origin = band.at[pl.ds(q * tile_lats + turn * part, part), pl.ds(2 * chip, 2)]
        return pltpu.make_async_remote_copy(
            src_ref=origin if root else here,
            dst_ref=here,
            send_sem=ring_send.at[turn, way, q, t],
            recv_sem=ring_recv.at[turn, way, q, t],
            device_id=(ring_to[turn], c),
            device_id_type=MESH,
        )

    def root_copy(way, q, t):
        chip = source_chip(way, t)
        return pltpu.make_async_copy(
            band.at[lats(q), pl.ds(2 * chip, 2)],
            panel.at[pl.ds((q - k * mine) * tile_lats, tile_lats), pl.ds(2 * chip, 2)],
            root_sem.at[way, q, t],
        )

    def chain_slot(i):
        q, t = slot_of(i)

        @pl.when(t == 0)
        def _():
            local(q).start()
            for way in range(2):
                @pl.when(has_next[way])
                def _(way=way):
                    chain(way, q, 0, True).start()
            pair(0, q, 0, True).start()

        for way in range(2):
            @pl.when(jnp.logical_and(t > 0, valid(way, t)))
            def _(way=way):
                chain(way, q, t - 1, False).wait_recv()

                @pl.when(has_next[way])
                def _():
                    chain(way, q, t, False).start()
                pair(way, q, t, False).start()

    def used(way, q, t):
        return jnp.logical_and(valid(way, t), q // mine == k)

    def root_slot(i):
        q, t = slot_of(i)
        for way in range(2):
            @pl.when(valid(way, t))
            def _(way=way):
                pair(way, q, t, False).wait_recv()

                @pl.when(jnp.logical_and(way == 0, t == 0))
                def _():
                    local(q).wait()

                @pl.when(q // mine == k)
                def _():
                    for turn in range(2):
                        ring(turn, way, q, t, True).start()
                    root_copy(way, q, t).start()

    def leaf_slot(turn, i):
        q, t = slot_of(i)
        for way in range(2):
            @pl.when(used(way, q, t))
            def _(way=way):
                ring(turn, way, q, t, False).wait_recv()

                @pl.when(hops[turn] < rows - 1)
                def _():
                    ring(turn, way, q, t, False).start()

    def within(i):
        return jnp.logical_and(i >= 0, i < slots)

    @pl.loop(0, slots + spread * (rows - 1))
    def _(i):
        @pl.when(i < slots)
        def _():
            chain_slot(i)

        @pl.when(jnp.logical_and(is_root, within(i - 1)))
        def _():
            root_slot(i - 1)

        for turn in range(2):
            late = i - spread * hops[turn]

            @pl.when(jnp.logical_and(jnp.logical_not(is_root), within(late)))
            def _(turn=turn, late=late):
                leaf_slot(turn, late)

    @pl.loop(0, slots)
    def _(i):
        q, t = slot_of(i)

        @pl.when(jnp.logical_and(t == 0, jnp.logical_not(is_root)))
        def _():
            local(q).wait()

        for way in range(2):
            @pl.when(jnp.logical_and(has_next[way], jnp.logical_or(valid(way, t), t == 0)))
            def _(way=way):
                chain(way, q, t, False).wait_send()

            @pl.when(valid(way, t))
            def _(way=way):
                pair(way, q, t, False).wait_send()

                @pl.when(jnp.logical_not(is_root))
                def _():
                    pair(way, q, t, False).wait_recv()

            @pl.when(used(way, q, t))
            def _(way=way):
                for turn in range(2):
                    @pl.when(jnp.logical_or(is_root, hops[turn] < rows - 1))
                    def _(turn=turn):
                        ring(turn, way, q, t, False).wait_send()

                @pl.when(is_root)
                def _():
                    root_copy(way, q, t).wait()


def gather(block, tile_lats, panel_lats):
    rows, cols = lax.axis_size("row"), lax.axis_size("col")
    chips = cols // 2
    lat_rows, lon_cols, maps = block.shape
    tiles = lat_rows // tile_lats
    sems = pltpu.SemaphoreType.DMA
    hbm = pl.BlockSpec(memory_space=pltpu.HBM)
    return pl.pallas_call(
        functools.partial(gather_kernel, rows, chips, tile_lats),
        out_shape=(
            jax.ShapeDtypeStruct((lat_rows, cols, lon_cols, maps), block.dtype),
            jax.ShapeDtypeStruct((panel_lats, cols, lon_cols, maps), block.dtype),
        ),
        in_specs=[hbm],
        out_specs=(hbm, hbm),
        scratch_shapes=[
            sems((tiles,)),
            sems((2, tiles, chips)),
            sems((2, tiles, chips)),
            sems((2, tiles, chips)),
            sems((2, tiles, chips)),
            sems((2, tiles, chips)),
            sems((2, 2, tiles, chips)),
            sems((2, 2, tiles, chips)),
        ],
        compiler_params=pltpu.CompilerParams(collective_id=0, has_side_effects=True),
        name="gather_maps",
    )(block)


def product_kernel(row_tile_count, col_tile_count, wide, left, right, out):
    strip, part = out.shape
    row = lax.axis_index("row") * row_tile_count + pl.program_id(0) * strip // TILE
    col = lax.axis_index("col") * col_tile_count + pl.program_id(1) * part // TILE
    keep = col >= row
    scale = 1.0 / left.shape[1]

    @pl.when(keep)
    def _():
        @pl.loop(0, part // wide)
        def _(j):
            to = pl.ds(pl.multiple_of(j * wide, wide), wide)
            at = pl.ds(pl.multiple_of(pl.program_id(1) * part + j * wide, wide), wide)
            acc = lax.dot_general(
                left[...], right[at, :], (((1,), (1,)), ((), ())),
                preferred_element_type=jnp.float32)
            out[:, to] = (acc * scale).astype(out.dtype)

    @pl.when(jnp.logical_not(keep))
    def _():
        out[...] = jnp.zeros_like(out)


def product(left, right):
    rows, maps = left.shape
    cols = right.shape[0]
    strip, part, wide = TILE // 2, TILE, TILE // 4
    return pl.pallas_call(
        functools.partial(product_kernel, rows // TILE, cols // TILE, wide),
        grid=(rows // strip, cols // part),
        out_shape=jax.ShapeDtypeStruct((rows, cols), jnp.bfloat16),
        in_specs=[
            pl.BlockSpec((strip, maps), lambda i, j: (i, 0)),
            pl.BlockSpec((cols, maps), lambda i, j: (0, 0), pipeline_mode=pl.Buffered(1)),
        ],
        out_specs=pl.BlockSpec((strip, part), lambda i, j: (i, j)),
        compiler_params=pltpu.CompilerParams(vmem_limit_bytes=VMEM_LIMIT),
        name="covariance_product",
    )(left, right)


def per_device(anomalies, kappa, members, months, land):
    lat_rows, lon_cols, maps = anomalies.shape
    row_index = lax.axis_index("row")
    lat_ids = row_index * lat_rows + jnp.arange(lat_rows, dtype=jnp.int32)
    phi = ((lat_ids.astype(jnp.float32) + 0.5) / LAT - 0.5) * math.pi
    lat_weight = jnp.sqrt(jnp.cos(phi))
    sea_weight = jnp.where(land == 1, 1.0, 0.5).astype(jnp.float32)
    cell_weight = sea_weight * lat_weight[:, None]
    groups = members * MONTHS + months
    onehot = (groups[:, None] == jnp.arange(GROUPS, dtype=jnp.int32)[None, :]).astype(jnp.float32)
    counts = jnp.maximum(jnp.sum(onehot, axis=0), 1.0)
    field = extended(anomalies, "col", 1, STEPS, True)
    field = extended(field, "row", 0, STEPS, False).astype(jnp.float32)
    coeff = extended(extended(kappa, "col", 1, STEPS, True), "row", 0, STEPS, False)
    coeff = coeff.astype(jnp.float32)[:, :, None]
    for step in range(STEPS):
        inner = field[1:-1, 1:-1]
        coeff = coeff[1:-1, 1:-1]
        beside = field[2:, 1:-1] + field[:-2, 1:-1] + (field[1:-1, 2:] + field[1:-1, :-2])
        field = inner + coeff * (beside - 4.0 * inner)
    block = centre_maps(field, cell_weight, onehot, counts)
    lon = lon_cols * lax.axis_size("col")
    panel_lats = lat_rows * lax.axis_size("row") // lax.axis_size("col")
    band, panel = gather(block, TILE // lon, panel_lats)
    return product(band.reshape(-1, maps), panel.reshape(-1, maps))


def solution(mesh):
    placed = (P("row", "col", None), P("row", "col"), P(), P(), P("row", "col"))
    return jax.shard_map(
        per_device, mesh=mesh, in_specs=placed, out_specs=P("row", "col"), check_vma=False
    )
```

```python
import functools
import math

import jax
import jax.numpy as jnp
from jax import lax
from jax.experimental import pallas as pl
from jax.experimental.pallas import tpu as pltpu
from jax.sharding import PartitionSpec as P

LAT = 128
MONTHS = 12
STEPS = 4
TILE = 2048
GROUPS = 96
MESH = pl.DeviceIdType.MESH


def extended(array, axis, dim, width, wrap):
    size, length = (lax.axis_size(axis), array.shape[dim])
    up = [(i, (i + 1) % size) for i in range(size if wrap else size - 1)]
    down = [(j, i) for i, j in up]
    last = lax.slice_in_dim(array, length - width, length, axis=dim)
    first = lax.slice_in_dim(array, 0, width, axis=dim)
    before = lax.ppermute(last, axis, up)
    after = lax.ppermute(first, axis, down)
    return jnp.concatenate([before, array, after], axis=dim)


def centre_maps(field, weights, onehot, counts):
    lat_rows, lon_cols, maps = field.shape
    flat = field.reshape(lat_rows * lon_cols, maps)
    sums = jnp.dot(flat, onehot, precision=lax.Precision.HIGHEST)
    back = jnp.dot(sums / counts, onehot.T, precision=lax.Precision.HIGHEST)
    centred = ((flat - back) * weights.reshape(lat_rows * lon_cols, 1)).astype(jnp.bfloat16)
    return centred.reshape(lat_rows, lon_cols, maps)


def ring_place(r, size):
    half = size // 2
    return jnp.where(r % 2 == 0, r // 2, size - 1 - r // 2), half


def ring_row(place, size):
    place = lax.rem(place + size, size)
    return jnp.where(place < size // 2, 2 * place, 2 * (size - 1 - place) + 1)


def gather_kernel(
    rows, chips, tile_lats, x, band, panel,
    local_sem, root_sem, chain_send, chain_recv, pair_send, pair_recv, ring_send, ring_recv,
):
    r = lax.axis_index("row")
    c = lax.axis_index("col")
    z = c // 2
    k = c % 2
    tiles = x.shape[0] // tile_lats
    mine = tiles // 2
    part = tile_lats // 2
    slots = tiles * chips
    spread = 2
    place, _ = ring_place(r, rows)
    root_place, _ = ring_place(z, rows)
    ring_to = (ring_row(place + 1, rows), ring_row(place - 1, rows))
    hops = (lax.rem(place - root_place + rows, rows), lax.rem(root_place - place + rows, rows))
    is_root = r == z
    has_next = (z < chips - 1, z > 0)
    step = (1, -1)

    def signal(row, col):
        pl.semaphore_signal(barrier, inc=1, device_id=(row, col), device_id_type=MESH)

    barrier = pltpu.get_barrier_semaphore()
    signal(r, 2 * z + 1 - k)
    signal(ring_to[0], c)
    signal(ring_to[1], c)
    for way in range(2):
        @pl.when(has_next[way])
        def _(way=way):
            signal(r, c + 2 * step[way])
    pl.semaphore_wait(
        barrier, 3 + has_next[0].astype(jnp.int32) + has_next[1].astype(jnp.int32))

    def slot_of(i):
        j = i % tiles
        return (j % 2) * mine + j // 2, i // tiles

    def lats(q):
        return pl.ds(q * tile_lats, tile_lats)

    def source_chip(way, t):
        return z - step[way] * t

    def valid(way, t):
        chip = source_chip(way, t)
        ok = jnp.logical_and(chip >= 0, chip < chips)
        return ok if way == 0 else jnp.logical_and(ok, t > 0)

    def local(q):
        return pltpu.make_async_copy(x.at[lats(q)], band.at[lats(q), c], local_sem.at[q])

    def block_copy(way, q, t, own, sems, target, piece):
        block = 2 * source_chip(way, t) + k
        first, count = piece
        at = pl.ds(q * tile_lats + first, count)
        return pltpu.make_async_remote_copy(
            src_ref=x.at[at] if own else band.at[at, block],
            dst_ref=band.at[at, block],
            send_sem=sems[0].at[way, q, t],
            recv_sem=sems[1].at[way, q, t],
            device_id=(r, target),
            device_id_type=MESH,
        )

    def chain(way, q, t, own=False, piece=(0, tile_lats)):
        sems = (chain_send, chain_recv)
        return block_copy(way, q, t, own, sems, c + 2 * step[way], piece)

    def pair(way, q, t, own=False, piece=(0, tile_lats)):
        return block_copy(way, q, t, own, (pair_send, pair_recv), 2 * z + 1 - k, piece)

    def ring(turn, way, q, t, root=False, piece=(0, part)):
        chip = source_chip(way, t)
        first, count = piece
        inside = turn * part + first
        here = panel.at[pl.ds((q - k * mine) * tile_lats + inside, count), pl.ds(2 * chip, 2)]
        origin = band.at[pl.ds(q * tile_lats + inside, count), pl.ds(2 * chip, 2)]
        return pltpu.make_async_remote_copy(
            src_ref=origin if root else here,
            dst_ref=here,
            send_sem=ring_send.at[turn, way, q, t],
            recv_sem=ring_recv.at[turn, way, q, t],
            device_id=(ring_to[turn], c),
            device_id_type=MESH,
        )

    def send(copy, size, *where):
        for first in range(size):
            copy(*where, piece=(first, 1)).start()

    def root_copy(way, q, t):
        chip = source_chip(way, t)
        return pltpu.make_async_copy(
            band.at[lats(q), pl.ds(2 * chip, 2)],
            panel.at[pl.ds((q - k * mine) * tile_lats, tile_lats), pl.ds(2 * chip, 2)],
            root_sem.at[way, q, t],
        )

    def chain_slot(i):
        q, t = slot_of(i)

        @pl.when(t == 0)
        def _():
            local(q).start()
            for way in range(2):
                @pl.when(has_next[way])
                def _(way=way):
                    send(chain, tile_lats, way, q, 0, True)
            send(pair, tile_lats, 0, q, 0, True)

        for way in range(2):
            @pl.when(jnp.logical_and(t > 0, valid(way, t)))
            def _(way=way):
                chain(way, q, t - 1, False).wait_recv()

                @pl.when(has_next[way])
                def _():
                    send(chain, tile_lats, way, q, t, False)
                send(pair, tile_lats, way, q, t, False)

    def used(way, q, t):
        return jnp.logical_and(valid(way, t), q // mine == k)

    def root_slot(i):
        q, t = slot_of(i)
        for way in range(2):
            @pl.when(valid(way, t))
            def _(way=way):
                pair(way, q, t, False).wait_recv()

                @pl.when(jnp.logical_and(way == 0, t == 0))
                def _():
                    local(q).wait()

                @pl.when(q // mine == k)
                def _():
                    for turn in range(2):
                        send(ring, part, turn, way, q, t, True)
                    root_copy(way, q, t).start()

    def leaf_slot(turn, i):
        q, t = slot_of(i)
        for way in range(2):
            @pl.when(used(way, q, t))
            def _(way=way):
                ring(turn, way, q, t, False).wait_recv()

                @pl.when(hops[turn] < rows - 1)
                def _():
                    send(ring, part, turn, way, q, t, False)

    def within(i):
        return jnp.logical_and(i >= 0, i < slots)

    @pl.loop(0, slots + spread * (rows - 1))
    def _(i):
        @pl.when(i < slots)
        def _():
            chain_slot(i)

        @pl.when(jnp.logical_and(is_root, within(i - 1)))
        def _():
            root_slot(i - 1)

        for turn in range(2):
            late = i - spread * hops[turn]

            @pl.when(jnp.logical_and(jnp.logical_not(is_root), within(late)))
            def _(turn=turn, late=late):
                leaf_slot(turn, late)

    @pl.loop(0, slots)
    def _(i):
        q, t = slot_of(i)

        @pl.when(jnp.logical_and(t == 0, jnp.logical_not(is_root)))
        def _():
            local(q).wait()

        for way in range(2):
            @pl.when(jnp.logical_and(has_next[way], jnp.logical_or(valid(way, t), t == 0)))
            def _(way=way):
                chain(way, q, t, False).wait_send()

            @pl.when(valid(way, t))
            def _(way=way):
                pair(way, q, t, False).wait_send()

                @pl.when(jnp.logical_not(is_root))
                def _():
                    pair(way, q, t, False).wait_recv()

            @pl.when(used(way, q, t))
            def _(way=way):
                for turn in range(2):
                    @pl.when(jnp.logical_or(is_root, hops[turn] < rows - 1))
                    def _(turn=turn):
                        ring(turn, way, q, t, False).wait_send()

                @pl.when(is_root)
                def _():
                    root_copy(way, q, t).wait()


def gather(block, tile_lats, panel_lats):
    rows, cols = lax.axis_size("row"), lax.axis_size("col")
    chips = cols // 2
    lat_rows, lon_cols, maps = block.shape
    tiles = lat_rows // tile_lats
    sems = pltpu.SemaphoreType.DMA
    hbm = pl.BlockSpec(memory_space=pltpu.HBM)
    return pl.pallas_call(
        functools.partial(gather_kernel, rows, chips, tile_lats),
        out_shape=(
            jax.ShapeDtypeStruct((lat_rows, cols, lon_cols, maps), block.dtype),
            jax.ShapeDtypeStruct((panel_lats, cols, lon_cols, maps), block.dtype),
        ),
        in_specs=[hbm],
        out_specs=(hbm, hbm),
        scratch_shapes=[
            sems((tiles,)),
            sems((2, tiles, chips)),
            sems((2, tiles, chips)),
            sems((2, tiles, chips)),
            sems((2, tiles, chips)),
            sems((2, tiles, chips)),
            sems((2, 2, tiles, chips)),
            sems((2, 2, tiles, chips)),
        ],
        compiler_params=pltpu.CompilerParams(collective_id=0, has_side_effects=True),
        name="gather_maps",
    )(block)


def product(left, right):
    rows, cols = left.shape[0], right.shape[0]
    row_tile = (lax.axis_index("row") * rows + jnp.arange(rows, dtype=jnp.int32)) // TILE
    col_tile = (lax.axis_index("col") * cols + jnp.arange(cols, dtype=jnp.int32)) // TILE
    whole = lax.dot_general(
        left, right, (((1,), (1,)), ((), ())), preferred_element_type=jnp.float32)
    whole = whole * (1.0 / left.shape[1])
    whole = jnp.where(col_tile[None, :] >= row_tile[:, None], whole, 0.0)
    return whole.astype(jnp.bfloat16)


def per_device(anomalies, kappa, members, months, land):
    lat_rows, lon_cols, maps = anomalies.shape
    row_index = lax.axis_index("row")
    lat_ids = row_index * lat_rows + jnp.arange(lat_rows, dtype=jnp.int32)
    phi = ((lat_ids.astype(jnp.float32) + 0.5) / LAT - 0.5) * math.pi
    lat_weight = jnp.sqrt(jnp.cos(phi))
    sea_weight = jnp.where(land == 1, 1.0, 0.5).astype(jnp.float32)
    cell_weight = sea_weight * lat_weight[:, None]
    groups = members * MONTHS + months
    onehot = (groups[:, None] == jnp.arange(GROUPS, dtype=jnp.int32)[None, :]).astype(jnp.float32)
    counts = jnp.maximum(jnp.sum(onehot, axis=0), 1.0)
    field = extended(anomalies, "col", 1, STEPS, True)
    field = extended(field, "row", 0, STEPS, False).astype(jnp.float32)
    coeff = extended(extended(kappa, "col", 1, STEPS, True), "row", 0, STEPS, False)
    coeff = coeff.astype(jnp.float32)[:, :, None]
    for step in range(STEPS):
        inner = field[1:-1, 1:-1]
        coeff = coeff[1:-1, 1:-1]
        beside = field[2:, 1:-1] + field[:-2, 1:-1] + (field[1:-1, 2:] + field[1:-1, :-2])
        field = inner + coeff * (beside - 4.0 * inner)
    block = centre_maps(field, cell_weight, onehot, counts)
    lon = lon_cols * lax.axis_size("col")
    panel_lats = lat_rows * lax.axis_size("row") // lax.axis_size("col")
    band, panel = gather(block, TILE // lon, panel_lats)
    return product(band.reshape(-1, maps), panel.reshape(-1, maps))


def solution(mesh):
    placed = (P("row", "col", None), P("row", "col"), P(), P(), P("row", "col"))
    return jax.shard_map(
        per_device, mesh=mesh, in_specs=placed, out_specs=P("row", "col"), check_vma=False
    )
```

```python
import functools
import math

import jax
import jax.numpy as jnp
from jax import lax
from jax.experimental import pallas as pl
from jax.experimental.pallas import tpu as pltpu
from jax.sharding import PartitionSpec as P

LAT = 128
MONTHS = 12
STEPS = 4
TILE = 2048
GROUPS = 96
MESH = pl.DeviceIdType.MESH


def extended(array, axis, dim, width, wrap):
    size, length = (lax.axis_size(axis), array.shape[dim])
    up = [(i, (i + 1) % size) for i in range(size if wrap else size - 1)]
    down = [(j, i) for i, j in up]
    last = lax.slice_in_dim(array, length - width, length, axis=dim)
    first = lax.slice_in_dim(array, 0, width, axis=dim)
    before = lax.ppermute(last, axis, up)
    after = lax.ppermute(first, axis, down)
    return jnp.concatenate([before, array, after], axis=dim)


def centre_maps(field, weights, onehot, counts):
    lat_rows, lon_cols, maps = field.shape
    flat = field.reshape(lat_rows * lon_cols, maps)
    sums = jnp.dot(flat, onehot, precision=lax.Precision.HIGHEST)
    back = jnp.dot(sums / counts, onehot.T, precision=lax.Precision.HIGHEST)
    centred = ((flat - back) * weights.reshape(lat_rows * lon_cols, 1)).astype(jnp.bfloat16)
    return centred.reshape(lat_rows, lon_cols, maps)


def ring_place(r, size):
    half = size // 2
    return jnp.where(r % 2 == 0, r // 2, size - 1 - r // 2), half


def ring_row(place, size):
    place = lax.rem(place + size, size)
    return jnp.where(place < size // 2, 2 * place, 2 * (size - 1 - place) + 1)


def gather_kernel(
    rows, chips, tile_lats, x, band, panel,
    local_sem, chain_send, chain_recv, pair_send, pair_recv, ring_send, ring_recv,
):
    r = lax.axis_index("row")
    c = lax.axis_index("col")
    z = c // 2
    k = c % 2
    tiles = x.shape[0] // tile_lats
    mine = tiles // 2
    part = tile_lats // 2
    slots = tiles * chips
    spread = 2
    place, _ = ring_place(r, rows)
    root_place, _ = ring_place(z, rows)
    ring_to = (ring_row(place + 1, rows), ring_row(place - 1, rows))
    hops = (lax.rem(place - root_place + rows, rows), lax.rem(root_place - place + rows, rows))
    is_root = r == z
    has_next = (z < chips - 1, z > 0)
    step = (1, -1)

    def signal(row, col):
        pl.semaphore_signal(barrier, inc=1, device_id=(row, col), device_id_type=MESH)

    barrier = pltpu.get_barrier_semaphore()
    signal(r, 2 * z + 1 - k)
    signal(ring_to[0], c)
    signal(ring_to[1], c)
    for way in range(2):
        @pl.when(has_next[way])
        def _(way=way):
            signal(r, c + 2 * step[way])
    pl.semaphore_wait(
        barrier, 3 + has_next[0].astype(jnp.int32) + has_next[1].astype(jnp.int32))

    def slot_of(i):
        j = i % tiles
        return (j % 2) * mine + j // 2, i // tiles

    def source_chip(way, t):
        return z - step[way] * t

    def valid(way, t):
        chip = source_chip(way, t)
        ok = jnp.logical_and(chip >= 0, chip < chips)
        return ok if way == 0 else jnp.logical_and(ok, t > 0)

    def local(q, piece=(0, tile_lats)):
        first, count = piece
        at = pl.ds(q * tile_lats + first, count)
        return pltpu.make_async_copy(x.at[at], band.at[at, c], local_sem.at[q])

    def block_copy(way, q, t, own, sems, target, piece):
        block = 2 * source_chip(way, t) + k
        first, count = piece
        at = pl.ds(q * tile_lats + first, count)
        return pltpu.make_async_remote_copy(
            src_ref=x.at[at] if own else band.at[at, block],
            dst_ref=band.at[at, block],
            send_sem=sems[0].at[way, q, t],
            recv_sem=sems[1].at[way, q, t],
            device_id=(r, target),
            device_id_type=MESH,
        )

    def chain(way, q, t, own=False, piece=(0, tile_lats)):
        sems = (chain_send, chain_recv)
        return block_copy(way, q, t, own, sems, c + 2 * step[way], piece)

    def pair(way, q, t, own=False, piece=(0, tile_lats)):
        return block_copy(way, q, t, own, (pair_send, pair_recv), 2 * z + 1 - k, piece)

    def ring(turn, way, q, t, root=False, piece=(0, part)):
        chip = source_chip(way, t)
        first, count = piece
        inside = turn * part + first
        here = panel.at[pl.ds((q - k * mine) * tile_lats + inside, count), pl.ds(2 * chip, 2)]
        origin = band.at[pl.ds(q * tile_lats + inside, count), pl.ds(2 * chip, 2)]
        return pltpu.make_async_remote_copy(
            src_ref=origin if root else here,
            dst_ref=here,
            send_sem=ring_send.at[turn, way, q, t],
            recv_sem=ring_recv.at[turn, way, q, t],
            device_id=(ring_to[turn], c),
            device_id_type=MESH,
        )

    def send(copy, size, *where):
        for first in range(size):
            copy(*where, piece=(first, 1)).start()

    def chain_slot(i):
        q, t = slot_of(i)

        @pl.when(t == 0)
        def _():
            send(local, tile_lats, q)
            for way in range(2):
                @pl.when(has_next[way])
                def _(way=way):
                    send(chain, tile_lats, way, q, 0, True)
            send(pair, tile_lats, 0, q, 0, True)

        for way in range(2):
            @pl.when(jnp.logical_and(t > 0, valid(way, t)))
            def _(way=way):
                chain(way, q, t - 1, False).wait_recv()

                @pl.when(has_next[way])
                def _():
                    send(chain, tile_lats, way, q, t, False)
                send(pair, tile_lats, way, q, t, False)

    def used(way, q, t):
        return jnp.logical_and(valid(way, t), q // mine == k)

    def root_slot(i):
        q, t = slot_of(i)
        for way in range(2):
            @pl.when(valid(way, t))
            def _(way=way):
                pair(way, q, t, False).wait_recv()

                @pl.when(jnp.logical_and(way == 0, t == 0))
                def _():
                    local(q).wait()

                @pl.when(q // mine == k)
                def _():
                    for turn in range(2):
                        send(ring, part, turn, way, q, t, True)

    def leaf_slot(turn, i):
        q, t = slot_of(i)
        for way in range(2):
            @pl.when(used(way, q, t))
            def _(way=way):
                ring(turn, way, q, t, False).wait_recv()

                @pl.when(hops[turn] < rows - 1)
                def _():
                    send(ring, part, turn, way, q, t, False)

    def within(i):
        return jnp.logical_and(i >= 0, i < slots)

    @pl.loop(0, slots + spread * (rows - 1))
    def _(i):
        @pl.when(i < slots)
        def _():
            chain_slot(i)

        @pl.when(jnp.logical_and(is_root, within(i - 1)))
        def _():
            root_slot(i - 1)

        for turn in range(2):
            late = i - spread * hops[turn]

            @pl.when(jnp.logical_and(jnp.logical_not(is_root), within(late)))
            def _(turn=turn, late=late):
                leaf_slot(turn, late)

    @pl.loop(0, slots)
    def _(i):
        q, t = slot_of(i)

        @pl.when(jnp.logical_and(t == 0, jnp.logical_not(is_root)))
        def _():
            local(q).wait()

        for way in range(2):
            @pl.when(jnp.logical_and(has_next[way], jnp.logical_or(valid(way, t), t == 0)))
            def _(way=way):
                chain(way, q, t, False).wait_send()

            @pl.when(valid(way, t))
            def _(way=way):
                pair(way, q, t, False).wait_send()

                @pl.when(jnp.logical_not(is_root))
                def _():
                    pair(way, q, t, False).wait_recv()

            @pl.when(used(way, q, t))
            def _(way=way):
                for turn in range(2):
                    @pl.when(jnp.logical_or(is_root, hops[turn] < rows - 1))
                    def _(turn=turn):
                        ring(turn, way, q, t, False).wait_send()


def gather(block, tile_lats, panel_lats):
    rows, cols = lax.axis_size("row"), lax.axis_size("col")
    chips = cols // 2
    lat_rows, lon_cols, maps = block.shape
    tiles = lat_rows // tile_lats
    sems = pltpu.SemaphoreType.DMA
    hbm = pl.BlockSpec(memory_space=pltpu.HBM)
    return pl.pallas_call(
        functools.partial(gather_kernel, rows, chips, tile_lats),
        out_shape=(
            jax.ShapeDtypeStruct((lat_rows, cols, lon_cols, maps), block.dtype),
            jax.ShapeDtypeStruct((panel_lats, cols, lon_cols, maps), block.dtype),
        ),
        in_specs=[hbm],
        out_specs=(hbm, hbm),
        scratch_shapes=[
            sems((tiles,)),
            sems((2, tiles, chips)),
            sems((2, tiles, chips)),
            sems((2, tiles, chips)),
            sems((2, tiles, chips)),
            sems((2, 2, tiles, chips)),
            sems((2, 2, tiles, chips)),
        ],
        compiler_params=pltpu.CompilerParams(collective_id=0, has_side_effects=True),
        name="gather_maps",
    )(block)


def product(left, right):
    rows, cols = left.shape[0], right.shape[0]
    row_tile = (lax.axis_index("row") * rows + jnp.arange(rows, dtype=jnp.int32)) // TILE
    col_tile = (lax.axis_index("col") * cols + jnp.arange(cols, dtype=jnp.int32)) // TILE
    whole = lax.dot_general(
        left, right, (((1,), (1,)), ((), ())), preferred_element_type=jnp.float32)
    whole = whole * (1.0 / left.shape[1])
    whole = jnp.where(col_tile[None, :] >= row_tile[:, None], whole, 0.0)
    return whole.astype(jnp.bfloat16)


def per_device(anomalies, kappa, members, months, land):
    lat_rows, lon_cols, maps = anomalies.shape
    row_index = lax.axis_index("row")
    lat_ids = row_index * lat_rows + jnp.arange(lat_rows, dtype=jnp.int32)
    phi = ((lat_ids.astype(jnp.float32) + 0.5) / LAT - 0.5) * math.pi
    lat_weight = jnp.sqrt(jnp.cos(phi))
    sea_weight = jnp.where(land == 1, 1.0, 0.5).astype(jnp.float32)
    cell_weight = sea_weight * lat_weight[:, None]
    groups = members * MONTHS + months
    onehot = (groups[:, None] == jnp.arange(GROUPS, dtype=jnp.int32)[None, :]).astype(jnp.float32)
    counts = jnp.maximum(jnp.sum(onehot, axis=0), 1.0)
    field = extended(anomalies, "col", 1, STEPS, True)
    field = extended(field, "row", 0, STEPS, False).astype(jnp.float32)
    coeff = extended(extended(kappa, "col", 1, STEPS, True), "row", 0, STEPS, False)
    coeff = coeff.astype(jnp.float32)[:, :, None]
    for step in range(STEPS):
        inner = field[1:-1, 1:-1]
        coeff = coeff[1:-1, 1:-1]
        beside = field[2:, 1:-1] + field[:-2, 1:-1] + (field[1:-1, 2:] + field[1:-1, :-2])
        field = inner + coeff * (beside - 4.0 * inner)
    block = centre_maps(field, cell_weight, onehot, counts)
    lon = lon_cols * lax.axis_size("col")
    panel_lats = lat_rows * lax.axis_size("row") // lax.axis_size("col")
    band, panel = gather(block, TILE // lon, panel_lats)
    col_index = lax.axis_index("col")
    ratio = lax.axis_size("col") // lax.axis_size("row")
    own_panel = lax.dynamic_slice_in_dim(band, col_index % ratio * panel_lats, panel_lats, 0)
    panel = jnp.where(col_index // ratio == row_index, own_panel, panel)
    return product(band.reshape(-1, maps), panel.reshape(-1, maps))


def solution(mesh):
    placed = (P("row", "col", None), P("row", "col"), P(), P(), P("row", "col"))
    return jax.shard_map(
        per_device, mesh=mesh, in_specs=placed, out_specs=P("row", "col"), check_vma=False
    )
```
